32 devices in a mesh: region: 4 (over x, core), dom: 8 (over z, y).
Axes of the slice: x: 2, y: 2, z: 4, core: 2. Of those that a mesh axis runs over, the one named last changes fastest.
Arguments:
- fine_latents: bfloat16 [65536, 256], P(('region', 'dom')), may hold values from -6 to 6
- edge_latents: bfloat16 [294912, 256], P(('region', 'dom')), may hold values from -6 to 6
- send_rows: int32 [8192], P(('region', 'dom')), may hold values from 0 to 2047
- edge_senders: int32 [294912], P(('region', 'dom')), may hold values from 0 to 2303
- edge_targets: int32 [294912], P(('region', 'dom')), may hold values from 0 to 2047
- cluster_ids: int32 [65536], P(('region', 'dom')), may hold values from 0 to 1023, as said below
- coarse_latents: bfloat16 [1024, 256], P(('region', 'dom')), may hold values from -6 to 6
- coarse_senders: int32 [16384], P(('region', 'dom')), may hold values from 0 to 1023, as said below
- coarse_targets: int32 [16384], P(('region', 'dom')), may hold values from 0 to 1023, as said below
- sender_weight: bfloat16 [256, 256], replicated, may hold values from -0.375 to 0.375
- target_weight: bfloat16 [256, 256], replicated, may hold values from -0.375 to 0.375
- edge_weight: bfloat16 [256, 256], replicated, may hold values from -0.375 to 0.375
- message_weight: bfloat16 [256, 256], replicated, may hold values from -0.375 to 0.375
- self_weight: bfloat16 [256, 256], replicated, may hold values from -0.375 to 0.375
- inflow_weight: bfloat16 [256, 256], replicated, may hold values from -0.375 to 0.375
- update_weight: bfloat16 [256, 256], replicated, may hold values from -0.375 to 0.375
- pooling_weight: bfloat16 [256, 256], replicated, may hold values from -0.046875 to 0.046875
- upper_sender: bfloat16 [256, 256], replicated, may hold values from -0.375 to 0.375
- upper_target: bfloat16 [256, 256], replicated, may hold values from -0.375 to 0.375
- upper_update: bfloat16 [256, 256], replicated, may hold values from -0.375 to 0.375
- lifting_weight: bfloat16 [256, 256], replicated, may hold values from -0.375 to 0.375
Outputs:
- fine_out: bfloat16 [65536, 256], P(('region', 'dom'))
- coarse_out: bfloat16 [1024, 256], P(('region', 'dom'))
The draws below stay inside these ranges and needn't reach their ends.
Inputs may be any that keep to these rules, and one draw needn't show every extreme that they name: `cluster_ids`: A fine node of partition p in region r has its coarse node in region r's block (r * 256 to (r + 1) * 256 - 1) or in the block of region (r + 2) modulo 4; cluster sizes are uneven. `coarse_senders`: the sender of a coarse edge held by device p of region r lies in region r's block of 256 coarse nodes. `coarse_targets`: the target of a coarse edge held by device p lies in p's own 32 coarse nodes, p * 32 to (p + 1) * 32 - 1.
All inputs are finite; a program needn't handle non-finite values.
Results may differ from the reference program's by a relative error of at most 0.0095.
Values may be sent and summed in bfloat16 or wider, within the bound.
A program may use at most 128 MiB of HBM per device.

```python
import jax
import jax.numpy as jnp
from jax import lax

D = 256
NODE_DEV = 2048
EDGE_DEV = 9216
HALO = 128
C_DEV = 32
CE_DEV = 512
NODES = 65536
EDGES = 294912
HALOS = 8192
BLOCK = 256
COARSE = 1024
N_REGION = 4
N_DOM = 8


def draw_cluster_ids(key, part):
    total = NODE_DEV * N_REGION * N_DOM
    position = jnp.arange(total, dtype=jnp.int32)
    region = position // NODE_DEV // N_DOM
    keys = jax.random.split(jax.random.fold_in(key, 11), 5)
    onward = (jax.random.randint(keys[0], (total,), 0, 5) < 2).astype(jnp.int32)
    target_region = (region + onward * (N_REGION // 2)) % N_REGION
    spread_pick = jax.random.randint(keys[1], (total,), 0, BLOCK)
    hot_start = jax.random.randint(keys[2], (N_REGION,), 0, BLOCK)
    hot_pick = (hot_start[target_region] + jax.random.randint(keys[3], (total,), 0, max(BLOCK // 8, 1))) % BLOCK
    choose_hot = jax.random.randint(keys[4], (total,), 0, 2) == 0
    within = jnp.where(choose_hot, hot_pick, spread_pick)
    return (target_region * BLOCK + within).astype(jnp.int32)


def draw_coarse_senders(key, part):
    total = CE_DEV * N_REGION * N_DOM
    position = jnp.arange(total, dtype=jnp.int32)
    region = position // CE_DEV // N_DOM
    within = jax.random.randint(jax.random.fold_in(key, 23), (total,), 0, BLOCK)
    return (region * BLOCK + within).astype(jnp.int32)


def draw_coarse_targets(key, part):
    total = CE_DEV * N_REGION * N_DOM
    position = jnp.arange(total, dtype=jnp.int32)
    device = position // CE_DEV
    within = jax.random.randint(jax.random.fold_in(key, 37), (total,), 0, C_DEV)
    return (device * C_DEV + within).astype(jnp.int32)


def place_ends(drawn, key, least, high):
    shape = drawn.shape
    place = [jax.random.randint(jax.random.fold_in(key, axis), (), 0, shape[axis]) for axis in range(len(shape))]
    drawn = drawn.at[tuple(place)].set(least)
    longest = shape.index(max(shape))
    place[longest] = (place[longest] + 1) % shape[longest]
    return drawn.at[tuple(place)].set(high)


def block_levels(own_key, extent, cuts, smallest, largest):
    def one(dim, shards_of):
        draws = jax.random.uniform(jax.random.fold_in(jax.random.fold_in(own_key, 6), dim), (shards_of,), jnp.float32, smallest / len(cuts), largest / len(cuts))
        return jnp.repeat(jnp.exp(draws), extent[dim] // shards_of).reshape((-1,) + (1,) * (len(extent) - dim - 1))

    loudness = one(*cuts[0])
    for cut in cuts[1:]:
        loudness = loudness * one(*cut)
    return loudness


def gaussian(stream_key, shape, width, bound, cuts=(), held_as=jnp.bfloat16):
    result = width * jax.random.normal(stream_key, shape, jnp.float32)
    if cuts:
        result = result * block_levels(stream_key, shape, cuts, -0.22, 0.18)
    return jnp.clip(result, -bound, bound).astype(held_as)


def setup_inputs(seed: int = 0) -> dict:
    seeds = jax.random.split(jax.random.key(seed), 22)
    return {
        "fine_latents": gaussian(seeds[0], (NODES, D), 1.0, 6.0, ((0, 32),)),
        "edge_latents": gaussian(seeds[1], (EDGES, D), 1.0, 6.0, ((0, 32),)),
        "send_rows": place_ends(jax.random.randint(seeds[2], (HALOS,), 0, NODE_DEV), jax.random.fold_in(seeds[2], 1), 0, NODE_DEV - 1).astype(jnp.int32),
        "edge_senders": place_ends(jax.random.randint(seeds[3], (EDGES,), 0, NODE_DEV + 2 * HALO), jax.random.fold_in(seeds[3], 1), 0, (NODE_DEV + 2 * HALO) - 1).astype(jnp.int32),
        "edge_targets": place_ends(jax.random.randint(seeds[4], (EDGES,), 0, NODE_DEV), jax.random.fold_in(seeds[4], 1), 0, NODE_DEV - 1).astype(jnp.int32),
        "cluster_ids": draw_cluster_ids(jax.random.fold_in(seeds[21], 71), 0),
        "coarse_latents": gaussian(seeds[6], (COARSE, D), 1.0, 6.0, ((0, 32),)),
        "coarse_senders": draw_coarse_senders(jax.random.fold_in(seeds[21], 71), 0),
        "coarse_targets": draw_coarse_targets(jax.random.fold_in(seeds[21], 71), 0),
        "sender_weight": gaussian(seeds[9], (D, D), D ** -0.5, 0.375),
        "target_weight": gaussian(seeds[10], (D, D), D ** -0.5, 0.375),
        "edge_weight": gaussian(seeds[11], (D, D), D ** -0.5, 0.375),
        "message_weight": gaussian(seeds[12], (D, D), D ** -0.5, 0.375),
        "self_weight": gaussian(seeds[13], (D, D), D ** -0.5, 0.375),
        "inflow_weight": gaussian(seeds[14], (D, D), D ** -0.5, 0.375),
        "update_weight": gaussian(seeds[15], (D, D), D ** -0.5, 0.375),
        "pooling_weight": gaussian(seeds[16], (D, D), (D * (NODE_DEV // C_DEV)) ** -0.5, 0.046875),
        "upper_sender": gaussian(seeds[17], (D, D), D ** -0.5, 0.375),
        "upper_target": gaussian(seeds[18], (D, D), D ** -0.5, 0.375),
        "upper_update": gaussian(seeds[19], (D, D), D ** -0.5, 0.375),
        "lifting_weight": gaussian(seeds[20], (D, D), D ** -0.5, 0.375),
    }


def normalize(values):
    centered = values - lax.optimization_barrier(jnp.mean(values, axis=-1, keepdims=True))
    variance = lax.optimization_barrier(jnp.mean(centered * centered, axis=-1, keepdims=True))
    return centered * lax.rsqrt(variance + 1e-05)

def pick_rows(latents, row_list):
    return jnp.take(latents, row_list, axis=0)

def refine(packed, weights):
    latents, lower_rows, upper_rows, edges_here, senders, targets = packed
    sender_weight, target_weight, edge_weight, message_weight, self_weight, inflow_weight, update_weight = weights
    extended = jnp.concatenate([latents, lower_rows, upper_rows], axis=0)
    from_side = jnp.dot(extended, sender_weight, preferred_element_type=jnp.float32).astype(jnp.bfloat16)
    to_side = jnp.dot(latents, target_weight, preferred_element_type=jnp.float32).astype(jnp.bfloat16)
    preact = jnp.take(from_side, senders, axis=0).astype(jnp.float32) + jnp.take(to_side, targets, axis=0).astype(jnp.float32)
    preact = preact + jnp.dot(edges_here, edge_weight, preferred_element_type=jnp.float32)
    hidden = jax.nn.silu(preact).astype(jnp.bfloat16)
    message = normalize(jnp.dot(hidden, message_weight, preferred_element_type=jnp.float32)).astype(jnp.bfloat16)
    inflow = jax.ops.segment_sum(message.astype(jnp.float32), targets, num_segments=latents.shape[0]).astype(jnp.bfloat16)
    node_hidden = jnp.dot(latents, self_weight, preferred_element_type=jnp.float32) + jnp.dot(inflow, inflow_weight, preferred_element_type=jnp.float32)
    node_hidden = jax.nn.silu(node_hidden).astype(jnp.bfloat16)
    update = normalize(jnp.dot(node_hidden, update_weight, preferred_element_type=jnp.float32))
    return (latents.astype(jnp.float32) + update).astype(jnp.bfloat16)

def reference(fine_latents, edge_latents, send_rows, edge_senders, edge_targets, cluster_ids, coarse_latents, coarse_senders, coarse_targets, sender_weight, target_weight, edge_weight, message_weight, self_weight, inflow_weight, update_weight, pooling_weight, upper_sender, upper_target, upper_update, lifting_weight):
    devices = N_REGION * N_DOM
    latents = fine_latents.reshape(N_REGION, N_DOM, NODE_DEV, D)
    row_lists = send_rows.reshape(N_REGION, N_DOM, 2 * HALO)
    exported = jax.vmap(jax.vmap(pick_rows))(latents, row_lists)
    zero_rows = jnp.zeros((N_REGION, 1, HALO, D), fine_latents.dtype)
    lower_rows = jnp.concatenate([zero_rows, exported[:, :-1, HALO:]], axis=1)
    upper_rows = jnp.concatenate([exported[:, 1:, :HALO], zero_rows], axis=1)
    weights = (sender_weight, target_weight, edge_weight, message_weight, self_weight, inflow_weight, update_weight)
    packed = (latents.reshape(devices, NODE_DEV, D), lower_rows.reshape(devices, HALO, D), upper_rows.reshape(devices, HALO, D), edge_latents.reshape(devices, EDGE_DEV, D), edge_senders.reshape(devices, EDGE_DEV), edge_targets.reshape(devices, EDGE_DEV))
    refined = lax.map(lambda item: refine(item, weights), packed).reshape(NODES, D)
    pooled = jax.ops.segment_sum(refined.astype(jnp.float32), cluster_ids, num_segments=COARSE).astype(jnp.bfloat16)
    coarse_start = (coarse_latents.astype(jnp.float32) + jnp.dot(pooled, pooling_weight, preferred_element_type=jnp.float32)).astype(jnp.bfloat16)
    upper_from = jnp.dot(coarse_start, upper_sender, preferred_element_type=jnp.float32).astype(jnp.bfloat16)
    upper_to = jnp.dot(coarse_start, upper_target, preferred_element_type=jnp.float32).astype(jnp.bfloat16)
    coarse_pre = jnp.take(upper_from, coarse_senders, axis=0).astype(jnp.float32) + jnp.take(upper_to, coarse_targets, axis=0).astype(jnp.float32)
    coarse_message = jax.nn.silu(coarse_pre).astype(jnp.bfloat16)
    coarse_inflow = jax.ops.segment_sum(coarse_message.astype(jnp.float32), coarse_targets, num_segments=COARSE).astype(jnp.bfloat16)
    coarse_update = normalize(jnp.dot(coarse_inflow, upper_update, preferred_element_type=jnp.float32))
    coarse_out = (coarse_start.astype(jnp.float32) + coarse_update).astype(jnp.bfloat16)
    lifted = jnp.dot(coarse_out, lifting_weight, preferred_element_type=jnp.float32).astype(jnp.bfloat16)
    fine_out = (refined.astype(jnp.float32) + jnp.take(lifted, cluster_ids, axis=0).astype(jnp.float32)).astype(jnp.bfloat16)
    return (fine_out, coarse_out)
```

```python
import functools

import jax
import jax.numpy as jnp
from jax import lax
from jax.experimental import pallas as pl
from jax.experimental.pallas import tpu as pltpu
from jax.sharding import PartitionSpec as P

EDGE_TILE = 512
NODE_TILE = 512
F32 = jnp.float32
BF16 = jnp.bfloat16


def normalize(values):
    centered = values - jnp.mean(values, axis=-1, keepdims=True)
    variance = jnp.mean(centered * centered, axis=-1, keepdims=True)
    return centered * lax.rsqrt(variance + 1e-05)


def silu(values):
    return values * pl.reciprocal(1.0 + jnp.exp(-values), approx=False)


def mm(a, b):
    return jnp.dot(a, b, preferred_element_type=F32)


def hot_columns(row, width):
    count = row.shape[1]
    spread = jnp.transpose(jnp.broadcast_to(row, (128, count))).astype(jnp.int16)
    lane = lax.broadcasted_iota(jnp.int32, (count, 128), 1).astype(jnp.int16)
    one = jnp.ones((count, 128), BF16)
    zero = jnp.zeros((count, 128), BF16)
    return [
        jnp.where(spread == lane + jnp.int16(k * 128), one, zero) for k in range(width // 128)
    ]


def hot_rows(row, first, height):
    count = row.shape[1]
    spread = jnp.broadcast_to(row - first, (height, count)).astype(jnp.int16)
    place = lax.broadcasted_iota(jnp.int32, (height, count), 0).astype(jnp.int16)
    return jnp.where(spread == place, jnp.ones((height, count), BF16), jnp.zeros((height, count), BF16))


def fine_kernel(
    edge_steps,
    fine_ref,
    halo_ref,
    edges_ref,
    senders_ref,
    targets_ref,
    window_ref,
    sender_w,
    target_w,
    edge_w,
    message_w,
    self_w,
    inflow_w,
    update_w,
    refined_ref,
    pooled_ref,
    table,
    messages,
):
    step = pl.program_id(0)
    nodes = fine_ref.shape[0]
    extended = nodes + halo_ref.shape[0]
    tile = edges_ref.shape[0]

    @pl.when(step == 0)
    def _():
        table[:nodes] = mm(fine_ref[...], sender_w[...]).astype(BF16)
        table[nodes:extended] = mm(halo_ref[...], sender_w[...]).astype(BF16)
        table[extended : extended + nodes] = mm(fine_ref[...], target_w[...]).astype(BF16)
        table[extended + nodes :] = edge_w[...]
        pooled_ref[...] = jnp.zeros_like(pooled_ref)

    @pl.when(step < edge_steps)
    def _():
        s_row = senders_ref[pl.ds(step, 1)]
        t_row = targets_ref[pl.ds(step, 1)]
        pieces = hot_columns(s_row, extended) + hot_columns(t_row, nodes) + [edges_ref[...]]
        hidden = silu(mm(jnp.concatenate(pieces, axis=1), table[...])).astype(BF16)
        messages[pl.ds(pl.multiple_of(step * tile, tile), tile)] = normalize(
            mm(hidden, message_w[...])
        ).astype(BF16)

    @pl.when(step >= edge_steps)
    def _():
        number = step - edge_steps
        first = pl.multiple_of(number * NODE_TILE, NODE_TILE)
        here = pl.ds(first, NODE_TILE)
        hot = jnp.concatenate(
            [hot_rows(targets_ref[k : k + 1], first, NODE_TILE) for k in range(edge_steps)], axis=1
        )
        inflow = mm(hot, messages[...]).astype(BF16)
        own = fine_ref[here]
        node_hidden = silu(mm(own, self_w[...]) + mm(inflow, inflow_w[...])).astype(BF16)
        refined = (own.astype(F32) + normalize(mm(node_hidden, update_w[...]))).astype(BF16)
        refined_ref[here] = refined
        pooled_ref[...] += mm(hot_rows(window_ref[pl.ds(number, 1)], 0, pooled_ref.shape[0]), refined)


def fine_stage(fine, halo, edges, senders, targets, window_ids, window, weights):
    nodes, depth = fine.shape
    count = edges.shape[0]
    edge_steps = count // EDGE_TILE
    node_steps = nodes // NODE_TILE
    whole = pl.BlockSpec(memory_space=pltpu.VMEM)
    return pl.pallas_call(
        functools.partial(fine_kernel, edge_steps),
        grid=(edge_steps + node_steps,),
        out_shape=(
            jax.ShapeDtypeStruct((nodes, depth), BF16),
            jax.ShapeDtypeStruct((window, depth), F32),
        ),
        in_specs=[
            whole,
            whole,
            pl.BlockSpec((EDGE_TILE, depth), lambda i: (jnp.minimum(i, edge_steps - 1), 0)),
        ]
        + [whole] * 10,
        out_specs=(whole, whole),
        scratch_shapes=[
            pltpu.VMEM((2 * nodes + halo.shape[0] + depth, depth), BF16),
            pltpu.VMEM((count, depth), BF16),
        ],
        compiler_params=pltpu.CompilerParams(
            dimension_semantics=("arbitrary",), vmem_limit_bytes=56 * 2**20
        ),
        cost_estimate=pl.CostEstimate(
            flops=2 * depth * count * (3 * nodes + 3 * depth), bytes_accessed=8 * 2**20, transcendentals=0
        ),
    )(
        fine,
        halo,
        edges,
        senders.reshape(edge_steps, EDGE_TILE),
        targets.reshape(edge_steps, EDGE_TILE),
        window_ids.reshape(node_steps, NODE_TILE),
        *weights,
    )


def hot(ids, count):
    return (ids[:, None] == jnp.arange(count, dtype=ids.dtype)[None, :]).astype(BF16)


def body(
    fine_latents,
    edge_latents,
    send_rows,
    edge_senders,
    edge_targets,
    cluster_ids,
    coarse_latents,
    coarse_senders,
    coarse_targets,
    sender_weight,
    target_weight,
    edge_weight,
    message_weight,
    self_weight,
    inflow_weight,
    update_weight,
    pooling_weight,
    upper_sender,
    upper_target,
    upper_update,
    lifting_weight,
):
    halo_width = send_rows.shape[0] // 2
    region_index = lax.axis_index("region")
    dom_index = lax.axis_index("dom")
    dom_count = lax.axis_size("dom")
    region_count = lax.axis_size("region")
    owned = coarse_latents.shape[0]
    block = dom_count * owned
    exported = mm(hot(send_rows, fine_latents.shape[0]), fine_latents).astype(BF16)
    up = [(i, i + 1) for i in range(dom_count - 1)]
    down = [(i + 1, i) for i in range(dom_count - 1)]
    halo = jnp.concatenate(
        [
            lax.ppermute(exported[halo_width:], "dom", up),
            lax.ppermute(exported[:halo_width], "dom", down),
        ],
        axis=0,
    )
    is_partner = (cluster_ids // block != region_index).astype(jnp.int32)
    window_ids = cluster_ids % block + is_partner * block
    refined, partial = fine_stage(
        fine_latents,
        halo,
        edge_latents,
        edge_senders,
        edge_targets,
        window_ids,
        2 * block,
        (
            sender_weight,
            target_weight,
            edge_weight,
            message_weight,
            self_weight,
            inflow_weight,
            update_weight,
        ),
    )
    across = [(i, (i + region_count // 2) % region_count) for i in range(region_count)]
    summed = partial[:block] + lax.ppermute(partial[block:], "region", across)
    pooled = lax.psum_scatter(summed, "dom", scatter_dimension=0, tiled=True).astype(BF16)
    coarse_start = (coarse_latents.astype(F32) + mm(pooled, pooling_weight)).astype(BF16)
    upper_from = mm(coarse_start, upper_sender).astype(BF16)
    upper_to = mm(coarse_start, upper_target).astype(BF16)
    region_from = lax.all_gather(upper_from, "dom", axis=0, tiled=True)
    sender_slots = coarse_senders - region_index * block
    target_slots = coarse_targets - (region_index * dom_count + dom_index) * owned
    target_hot = hot(target_slots, owned)
    coarse_pre = mm(hot(sender_slots, block), region_from) + mm(target_hot, upper_to)
    coarse_message = jax.nn.silu(coarse_pre).astype(BF16)
    coarse_inflow = mm(target_hot.T, coarse_message).astype(BF16)
    coarse_update = normalize(mm(coarse_inflow, upper_update))
    coarse_out = (coarse_start.astype(F32) + coarse_update).astype(BF16)
    lifted = mm(coarse_out, lifting_weight).astype(BF16)
    region_lifted = lax.all_gather(lifted, "dom", axis=0, tiled=True)
    partner_lifted = lax.ppermute(region_lifted, "region", across)
    window_lifted = jnp.concatenate([region_lifted, partner_lifted], axis=0)
    fine_out = (refined.astype(F32) + mm(hot(window_ids, 2 * block), window_lifted)).astype(BF16)
    return (fine_out, coarse_out)


def solution(mesh):
    return jax.shard_map(
        body,
        mesh=mesh,
        in_specs=(
            P(("region", "dom"), None),
            P(("region", "dom"), None),
            P(("region", "dom")),
            P(("region", "dom")),
            P(("region", "dom")),
            P(("region", "dom")),
            P(("region", "dom"), None),
            P(("region", "dom")),
            P(("region", "dom")),
            P(),
            P(),
            P(),
            P(),
            P(),
            P(),
            P(),
            P(),
            P(),
            P(),
            P(),
            P(),
        ),
        out_specs=(P(("region", "dom"), None), P(("region", "dom"), None)),
        check_vma=False,
    )
```

```python
import functools

import jax
import jax.numpy as jnp
from jax import lax
from jax.experimental import pallas as pl
from jax.experimental.pallas import tpu as pltpu
from jax.sharding import PartitionSpec as P

EDGE_TILE = 512
NODE_TILE = 512
F32 = jnp.float32
BF16 = jnp.bfloat16


def normalize(values):
    centered = values - jnp.mean(values, axis=-1, keepdims=True)
    variance = jnp.mean(centered * centered, axis=-1, keepdims=True)
    return centered * lax.rsqrt(variance + 1e-05)


def silu(values):
    return values * pl.reciprocal(1.0 + jnp.exp(-values), approx=False)


def mm(a, b):
    return jnp.dot(a, b, preferred_element_type=F32)


def hot_columns(row, width):
    count = row.shape[1]
    spread = jnp.transpose(jnp.broadcast_to(row, (128, count))).astype(jnp.int16)
    lane = lax.broadcasted_iota(jnp.int32, (count, 128), 1).astype(jnp.int16)
    one = jnp.ones((count, 128), BF16)
    zero = jnp.zeros((count, 128), BF16)
    return [
        jnp.where(spread == lane + jnp.int16(k * 128), one, zero) for k in range(width // 128)
    ]


def hot_rows(row, first, height):
    count = row.shape[1]
    spread = jnp.broadcast_to(row - first, (height, count)).astype(jnp.int16)
    place = lax.broadcasted_iota(jnp.int32, (height, count), 0).astype(jnp.int16)
    return jnp.where(spread == place, jnp.ones((height, count), BF16), jnp.zeros((height, count), BF16))


def fine_kernel(
    edge_steps,
    fine_ref,
    halo_ref,
    edges_ref,
    senders_ref,
    targets_ref,
    window_ref,
    sender_w,
    target_w,
    edge_w,
    message_w,
    self_w,
    inflow_w,
    update_w,
    refined_ref,
    pooled_ref,
    table,
    messages,
    pooled,
):
    step = pl.program_id(0)
    nodes = fine_ref.shape[0]
    extended = nodes + halo_ref.shape[0]
    tile = edges_ref.shape[0]

    @pl.when(step == 0)
    def _():
        table[:nodes] = mm(fine_ref[...], sender_w[...]).astype(BF16)
        table[nodes:extended] = mm(halo_ref[...], sender_w[...]).astype(BF16)
        table[extended : extended + nodes] = mm(fine_ref[...], target_w[...]).astype(BF16)
        table[extended + nodes :] = edge_w[...]
        pooled[...] = jnp.zeros_like(pooled)

    @pl.when(step < edge_steps)
    def _():
        s_row = senders_ref[pl.ds(step, 1)]
        t_row = targets_ref[pl.ds(step, 1)]
        pieces = hot_columns(s_row, extended) + hot_columns(t_row, nodes) + [edges_ref[...]]
        hidden = silu(mm(jnp.concatenate(pieces, axis=1), table[...])).astype(BF16)
        messages[pl.ds(pl.multiple_of(step * tile, tile), tile)] = normalize(
            mm(hidden, message_w[...])
        ).astype(BF16)

    @pl.when(step >= edge_steps)
    def _():
        number = step - edge_steps
        first = pl.multiple_of(number * NODE_TILE, NODE_TILE)
        here = pl.ds(first, NODE_TILE)
        hot = jnp.concatenate(
            [hot_rows(targets_ref[k : k + 1], first, NODE_TILE) for k in range(edge_steps)], axis=1
        )
        inflow = mm(hot, messages[...]).astype(BF16)
        own = fine_ref[here]
        node_hidden = silu(mm(own, self_w[...]) + mm(inflow, inflow_w[...])).astype(BF16)
        refined = (own.astype(F32) + normalize(mm(node_hidden, update_w[...]))).astype(BF16)
        refined_ref[here] = refined
        pooled[...] += mm(hot_rows(window_ref[pl.ds(number, 1)], 0, pooled.shape[0]), refined)

    @pl.when(step == pl.num_programs(0) - 1)
    def _():
        pooled_ref[...] = pooled[...].astype(BF16)


def fine_stage(fine, halo, edges, senders, targets, window_ids, window, weights):
    nodes, depth = fine.shape
    count = edges.shape[0]
    edge_steps = count // EDGE_TILE
    node_steps = nodes // NODE_TILE
    whole = pl.BlockSpec(memory_space=pltpu.VMEM)
    return pl.pallas_call(
        functools.partial(fine_kernel, edge_steps),
        grid=(edge_steps + node_steps,),
        out_shape=(
            jax.ShapeDtypeStruct((nodes, depth), BF16),
            jax.ShapeDtypeStruct((window, depth), BF16),
        ),
        in_specs=[
            whole,
            whole,
            pl.BlockSpec((EDGE_TILE, depth), lambda i: (jnp.minimum(i, edge_steps - 1), 0)),
        ]
        + [whole] * 10,
        out_specs=(whole, whole),
        scratch_shapes=[
            pltpu.VMEM((2 * nodes + halo.shape[0] + depth, depth), BF16),
            pltpu.VMEM((count, depth), BF16),
            pltpu.VMEM((window, depth), F32),
        ],
        compiler_params=pltpu.CompilerParams(
            dimension_semantics=("arbitrary",), vmem_limit_bytes=56 * 2**20
        ),
        cost_estimate=pl.CostEstimate(
            flops=2 * depth * count * (3 * nodes + 3 * depth), bytes_accessed=8 * 2**20, transcendentals=0
        ),
    )(
        fine,
        halo,
        edges,
        senders.reshape(edge_steps, EDGE_TILE),
        targets.reshape(edge_steps, EDGE_TILE),
        window_ids.reshape(node_steps, NODE_TILE),
        *weights,
    )


def to_device(src, dst, sends, receives, slot, region, dom):
    return pltpu.make_async_remote_copy(
        src_ref=src,
        dst_ref=dst,
        send_sem=sends.at[slot],
        recv_sem=receives.at[slot],
        device_id=(region, dom),
        device_id_type=pl.DeviceIdType.MESH,
    )


def halo_kernel(doms, fine_ref, rows_ref, halo_ref, exported, landed, sends, receives):
    region, me = lax.axis_index("region"), lax.axis_index("dom")
    above, below = lax.rem(me + 1, doms), lax.rem(me + doms - 1, doms)
    barrier = pltpu.get_barrier_semaphore()
    for other in (above, below):
        pl.semaphore_signal(
            barrier, inc=1, device_id=(region, other), device_id_type=pl.DeviceIdType.MESH
        )
    width = rows_ref.shape[1] // 2
    hot = jnp.concatenate(hot_columns(rows_ref[...], fine_ref.shape[0]), axis=1)
    exported[...] = mm(hot, fine_ref[...]).astype(BF16)
    pl.semaphore_wait(barrier, 2)
    lower, upper = pl.ds(0, width), pl.ds(width, width)
    copies = [
        to_device(exported.at[upper], landed.at[lower], sends, receives, 0, region, above),
        to_device(exported.at[lower], landed.at[upper], sends, receives, 1, region, below),
    ]
    for copy in copies:
        copy.start()
    for copy in copies:
        copy.wait()
    zeros = jnp.zeros((width, fine_ref.shape[1]), BF16)
    halo_ref[lower] = jnp.where(me > 0, landed[lower], zeros)
    halo_ref[upper] = jnp.where(me < doms - 1, landed[upper], zeros)


def halo_stage(fine, send_rows, doms):
    whole = pl.BlockSpec(memory_space=pltpu.VMEM)
    shape = (send_rows.shape[0], fine.shape[1])
    return pl.pallas_call(
        functools.partial(halo_kernel, doms),
        out_shape=jax.ShapeDtypeStruct(shape, BF16),
        in_specs=[whole] * 2,
        out_specs=whole,
        scratch_shapes=[
            pltpu.VMEM(shape, BF16),
            pltpu.VMEM(shape, BF16),
            pltpu.SemaphoreType.DMA((2,)),
            pltpu.SemaphoreType.DMA((2,)),
        ],
        compiler_params=pltpu.CompilerParams(
            collective_id=0, has_side_effects=True, vmem_limit_bytes=32 * 2**20
        ),
    )(fine, send_rows.reshape(1, -1))


def coarse_kernel(
    regions,
    doms,
    partial_ref,
    refined_ref,
    latents_ref,
    senders_ref,
    targets_ref,
    window_ref,
    pooling_w,
    sender_w,
    target_w,
    update_w,
    lifting_w,
    fine_ref,
    coarse_ref,
    arrived,
    region_from,
    lifted,
    chosen,
    picked,
    pool_send,
    pool_recv,
    from_send,
    from_recv,
    lift_send,
    lift_recv,
):
    region, me = lax.axis_index("region"), lax.axis_index("dom")
    partner = lax.rem(region + regions // 2, regions)
    owned = latents_ref.shape[0]
    block = doms * owned

    def part(dom, base=0):
        return pl.ds(base + pl.multiple_of(dom * owned, owned), owned)

    peers = [lax.rem(me + k, doms) for k in range(doms)]
    barrier = pltpu.get_barrier_semaphore()
    for k in range(doms):
        if k:
            pl.semaphore_signal(
                barrier, inc=1, device_id=(region, peers[k]), device_id_type=pl.DeviceIdType.MESH
            )
        pl.semaphore_signal(
            barrier, inc=1, device_id=(partner, peers[k]), device_id_type=pl.DeviceIdType.MESH
        )
    pl.semaphore_wait(barrier, 2 * doms - 1)

    pool = []
    for k in range(doms):
        pool.append(
            to_device(
                partial_ref.at[part(peers[k], block)],
                arrived.at[doms + k],
                pool_send,
                pool_recv,
                doms + k,
                partner,
                peers[k],
            )
        )
        if k:
            pool.append(
                to_device(
                    partial_ref.at[part(peers[k])],
                    arrived.at[k],
                    pool_send,
                    pool_recv,
                    k,
                    region,
                    peers[k],
                )
            )
    for copy in pool:
        copy.start()
    picked[...] = jnp.concatenate(hot_columns(senders_ref[...], block), axis=1)
    for n in range(window_ref.shape[0]):
        chosen[pl.ds(n * NODE_TILE, NODE_TILE)] = jnp.concatenate(
            hot_columns(window_ref[n : n + 1], 2 * block), axis=1
        )
    target_row = hot_rows(targets_ref[...], 0, owned)
    total = partial_ref[part(me)].astype(F32)
    for copy in pool:
        copy.wait_recv()
    for k in range(1, 2 * doms):
        total = total + arrived[k].astype(F32)
    start = (latents_ref[...].astype(F32) + mm(total.astype(BF16), pooling_w[...])).astype(BF16)
    region_from[part(me)] = mm(start, sender_w[...]).astype(BF16)
    shares = [
        to_device(
            region_from.at[part(me)], region_from.at[part(me)], from_send, from_recv, k, region, peers[k]
        )
        for k in range(1, doms)
    ]
    for copy in shares:
        copy.start()
    upper_to = mm(start, target_w[...]).astype(BF16)
    to_rows = lax.dot_general(
        target_row, upper_to, (((0,), (0,)), ((), ())), preferred_element_type=F32
    )
    for copy in shares:
        copy.wait_recv()
    message = silu(mm(picked[...], region_from[...]) + to_rows).astype(BF16)
    inflow = mm(target_row, message).astype(BF16)
    result = (start.astype(F32) + normalize(mm(inflow, update_w[...]))).astype(BF16)
    coarse_ref[...] = result
    lifted[part(me)] = mm(result, lifting_w[...]).astype(BF16)
    lifts = []
    for k in range(doms):
        lifts.append(
            to_device(
                lifted.at[part(me)],
                lifted.at[part(me, block)],
                lift_send,
                lift_recv,
                doms + k,
                partner,
                peers[k],
            )
        )
        if k:
            lifts.append(
                to_device(
                    lifted.at[part(me)], lifted.at[part(me)], lift_send, lift_recv, k, region, peers[k]
                )
            )
    for copy in lifts:
        copy.start()
    for copy in pool + shares:
        copy.wait_send()
    for copy in lifts:
        copy.wait_recv()
    for n in range(window_ref.shape[0]):
        rows = pl.ds(n * NODE_TILE, NODE_TILE)
        fine_ref[rows] = (
            refined_ref[rows].astype(F32) + mm(chosen[rows], lifted[...])
        ).astype(BF16)
    for copy in lifts:
        copy.wait_send()


def coarse_stage(partial, refined, latents, senders, targets, window_ids, weights, regions, doms):
    whole = pl.BlockSpec(memory_space=pltpu.VMEM)
    nodes, depth = refined.shape
    owned = latents.shape[0]
    block = doms * owned
    count = senders.shape[0]
    pair = [pltpu.SemaphoreType.DMA((2 * doms,))] * 2
    return pl.pallas_call(
        functools.partial(coarse_kernel, regions, doms),
        out_shape=(
            jax.ShapeDtypeStruct((nodes, depth), BF16),
            jax.ShapeDtypeStruct((owned, depth), BF16),
        ),
        in_specs=[whole] * 11,
        out_specs=(whole, whole),
        scratch_shapes=[
            pltpu.VMEM((2 * doms, owned, depth), BF16),
            pltpu.VMEM((block, depth), BF16),
            pltpu.VMEM((2 * block, depth), BF16),
            pltpu.VMEM((nodes, 2 * block), BF16),
            pltpu.VMEM((count, block), BF16),
        ]
        + pair * 3,
        compiler_params=pltpu.CompilerParams(
            collective_id=1, has_side_effects=True, vmem_limit_bytes=48 * 2**20
        ),
    )(
        partial,
        refined,
        latents,
        senders.reshape(1, -1),
        targets.reshape(1, -1),
        window_ids.reshape(-1, NODE_TILE),
        *weights,
    )


def body(
    fine_latents,
    edge_latents,
    send_rows,
    edge_senders,
    edge_targets,
    cluster_ids,
    coarse_latents,
    coarse_senders,
    coarse_targets,
    sender_weight,
    target_weight,
    edge_weight,
    message_weight,
    self_weight,
    inflow_weight,
    update_weight,
    pooling_weight,
    upper_sender,
    upper_target,
    upper_update,
    lifting_weight,
):
    region_index = lax.axis_index("region")
    dom_index = lax.axis_index("dom")
    dom_count = lax.axis_size("dom")
    region_count = lax.axis_size("region")
    owned = coarse_latents.shape[0]
    block = dom_count * owned
    halo = halo_stage(fine_latents, send_rows, dom_count)
    is_partner = (cluster_ids // block != region_index).astype(jnp.int32)
    window_ids = cluster_ids % block + is_partner * block
    refined, partial = fine_stage(
        fine_latents,
        halo,
        edge_latents,
        edge_senders,
        edge_targets,
        window_ids,
        2 * block,
        (
            sender_weight,
            target_weight,
            edge_weight,
            message_weight,
            self_weight,
            inflow_weight,
            update_weight,
        ),
    )
    fine_out, coarse_out = coarse_stage(
        partial,
        refined,
        coarse_latents,
        coarse_senders - region_index * block,
        coarse_targets - (region_index * dom_count + dom_index) * owned,
        window_ids,
        (pooling_weight, upper_sender, upper_target, upper_update, lifting_weight),
        region_count,
        dom_count,
    )
    return (fine_out, coarse_out)


def solution(mesh):
    return jax.shard_map(
        body,
        mesh=mesh,
        in_specs=(
            P(("region", "dom"), None),
            P(("region", "dom"), None),
            P(("region", "dom")),
            P(("region", "dom")),
            P(("region", "dom")),
            P(("region", "dom")),
            P(("region", "dom"), None),
            P(("region", "dom")),
            P(("region", "dom")),
            P(),
            P(),
            P(),
            P(),
            P(),
            P(),
            P(),
            P(),
            P(),
            P(),
            P(),
            P(),
        ),
        out_specs=(P(("region", "dom"), None), P(("region", "dom"), None)),
        check_vma=False,
    )
```

```python
import functools

import jax
import jax.numpy as jnp
from jax import lax
from jax.experimental import pallas as pl
from jax.experimental.pallas import tpu as pltpu
from jax.sharding import PartitionSpec as P

EDGE_TILE = 1024
NODE_TILE = 1024
F32 = jnp.float32
BF16 = jnp.bfloat16


def normalize(values):
    centered = values - jnp.mean(values, axis=-1, keepdims=True)
    variance = jnp.mean(centered * centered, axis=-1, keepdims=True)
    return centered * lax.rsqrt(variance + 1e-05)


def silu(values):
    return values * (0.5 + 0.5 * jnp.tanh(0.5 * values))


def mm(a, b):
    return jnp.dot(a, b, preferred_element_type=F32)


def hot_columns(row, width):
    count = row.shape[1]
    spread = jnp.transpose(jnp.broadcast_to(row, (128, count))).astype(jnp.int16)
    lane = lax.broadcasted_iota(jnp.int32, (count, 128), 1).astype(jnp.int16)
    one = jnp.ones((count, 128), BF16)
    zero = jnp.zeros((count, 128), BF16)
    return [
        jnp.where(spread == lane + jnp.int16(k * 128), one, zero) for k in range(width // 128)
    ]


def hot_rows(row, first, height):
    count = row.shape[1]
    spread = jnp.broadcast_to(row - first, (height, count)).astype(jnp.int16)
    place = lax.broadcasted_iota(jnp.int32, (height, count), 0).astype(jnp.int16)
    return jnp.where(spread == place, jnp.ones((height, count), BF16), jnp.zeros((height, count), BF16))


def in_window(clusters, block):
    within = clusters - lax.axis_index("region") * block
    own = (within >= 0) & (within < block)
    half = lax.axis_size("region") // 2 * block
    return jnp.where(own, within, block + within + jnp.where(within < 0, half, -half))


def fine_kernel(
    edge_steps,
    fine_ref,
    halo_ref,
    edges_ref,
    senders_ref,
    targets_ref,
    window_ref,
    sender_w,
    target_w,
    edge_w,
    message_w,
    self_w,
    inflow_w,
    update_w,
    refined_ref,
    pooled_ref,
    table,
    messages,
    pooled,
):
    step = pl.program_id(0)
    nodes = fine_ref.shape[0]
    extended = nodes + halo_ref.shape[0]
    tile = edges_ref.shape[0]

    @pl.when(step == 0)
    def _():
        table[:nodes] = mm(fine_ref[...], sender_w[...]).astype(BF16)
        table[nodes:extended] = mm(halo_ref[...], sender_w[...]).astype(BF16)
        table[extended : extended + nodes] = mm(fine_ref[...], target_w[...]).astype(BF16)
        table[extended + nodes :] = edge_w[...]
        pooled[...] = jnp.zeros_like(pooled)

    @pl.when(step < edge_steps)
    def _():
        here = pl.ds(pl.multiple_of(step * tile, tile), tile)
        s_row = senders_ref[here].reshape(1, tile)
        t_row = targets_ref[here].reshape(1, tile)
        pieces = hot_columns(s_row, extended) + hot_columns(t_row, nodes) + [edges_ref[...]]
        hidden = silu(mm(jnp.concatenate(pieces, axis=1), table[...])).astype(BF16)
        messages[here] = normalize(
            mm(hidden, message_w[...])
        ).astype(BF16)

    @pl.when(step >= edge_steps)
    def _():
        number = step - edge_steps
        first = pl.multiple_of(number * NODE_TILE, NODE_TILE)
        here = pl.ds(first, NODE_TILE)
        hot = jnp.concatenate(
            [
                hot_rows(targets_ref[pl.ds(k * tile, tile)].reshape(1, tile), first, NODE_TILE)
                for k in range(edge_steps)
            ],
            axis=1,
        )
        inflow = mm(hot, messages[...]).astype(BF16)
        own = fine_ref[here]
        node_hidden = silu(mm(own, self_w[...]) + mm(inflow, inflow_w[...])).astype(BF16)
        refined = (own.astype(F32) + normalize(mm(node_hidden, update_w[...]))).astype(BF16)
        refined_ref[here] = refined
        slots = in_window(window_ref[here].reshape(1, NODE_TILE), pooled.shape[0] // 2)
        pooled[...] += mm(hot_rows(slots, 0, pooled.shape[0]), refined)

    @pl.when(step == pl.num_programs(0) - 1)
    def _():
        pooled_ref[...] = pooled[...].astype(BF16)


def fine_stage(fine, halo, edges, senders, targets, window_ids, window, weights):
    nodes, depth = fine.shape
    count = edges.shape[0]
    edge_steps = count // EDGE_TILE
    node_steps = nodes // NODE_TILE
    whole = pl.BlockSpec(memory_space=pltpu.VMEM)
    return pl.pallas_call(
        functools.partial(fine_kernel, edge_steps),
        grid=(edge_steps + node_steps,),
        out_shape=(
            jax.ShapeDtypeStruct((nodes, depth), BF16),
            jax.ShapeDtypeStruct((window, depth), BF16),
        ),
        in_specs=[
            whole,
            whole,
            pl.BlockSpec((EDGE_TILE, depth), lambda i: (jnp.minimum(i, edge_steps - 1), 0)),
        ]
        + [whole] * 10,
        out_specs=(whole, whole),
        scratch_shapes=[
            pltpu.VMEM((2 * nodes + halo.shape[0] + depth, depth), BF16),
            pltpu.VMEM((count, depth), BF16),
            pltpu.VMEM((window, depth), F32),
        ],
        compiler_params=pltpu.CompilerParams(
            dimension_semantics=("arbitrary",), vmem_limit_bytes=56 * 2**20
        ),
        cost_estimate=pl.CostEstimate(
            flops=2 * depth * count * (3 * nodes + 3 * depth), bytes_accessed=8 * 2**20, transcendentals=0
        ),
    )(
        fine,
        halo,
        edges,
        senders,
        targets,
        window_ids,
        *weights,
    )


def to_device(src, dst, sends, receives, slot, region, dom):
    return pltpu.make_async_remote_copy(
        src_ref=src,
        dst_ref=dst,
        send_sem=sends.at[slot],
        recv_sem=receives.at[slot],
        device_id=(region, dom),
        device_id_type=pl.DeviceIdType.MESH,
    )


def halo_kernel(doms, fine_ref, rows_ref, halo_ref, exported, landed, sends, receives):
    region, me = lax.axis_index("region"), lax.axis_index("dom")
    above, below = lax.rem(me + 1, doms), lax.rem(me + doms - 1, doms)
    barrier = pltpu.get_barrier_semaphore()
    for other in (above, below):
        pl.semaphore_signal(
            barrier, inc=1, device_id=(region, other), device_id_type=pl.DeviceIdType.MESH
        )
    width = rows_ref.shape[0] // 2
    hot = jnp.concatenate(hot_columns(rows_ref[...].reshape(1, -1), fine_ref.shape[0]), axis=1)
    exported[...] = mm(hot, fine_ref[...]).astype(BF16)
    pl.semaphore_wait(barrier, 2)
    lower, upper = pl.ds(0, width), pl.ds(width, width)
    copies = [
        to_device(exported.at[upper], landed.at[lower], sends, receives, 0, region, above),
        to_device(exported.at[lower], landed.at[upper], sends, receives, 1, region, below),
    ]
    for copy in copies:
        copy.start()
    for copy in copies:
        copy.wait()
    zeros = jnp.zeros((width, fine_ref.shape[1]), BF16)
    halo_ref[lower] = jnp.where(me > 0, landed[lower], zeros)
    halo_ref[upper] = jnp.where(me < doms - 1, landed[upper], zeros)


def halo_stage(fine, send_rows, doms):
    whole = pl.BlockSpec(memory_space=pltpu.VMEM)
    shape = (send_rows.shape[0], fine.shape[1])
    return pl.pallas_call(
        functools.partial(halo_kernel, doms),
        out_shape=jax.ShapeDtypeStruct(shape, BF16),
        in_specs=[whole] * 2,
        out_specs=whole,
        scratch_shapes=[
            pltpu.VMEM(shape, BF16),
            pltpu.VMEM(shape, BF16),
            pltpu.SemaphoreType.DMA((2,)),
            pltpu.SemaphoreType.DMA((2,)),
        ],
        compiler_params=pltpu.CompilerParams(
            collective_id=0, has_side_effects=True, vmem_limit_bytes=32 * 2**20
        ),
    )(fine, send_rows)


def coarse_kernel(
    regions,
    doms,
    partial_ref,
    refined_ref,
    latents_ref,
    senders_ref,
    targets_ref,
    window_ref,
    pooling_w,
    sender_w,
    target_w,
    update_w,
    lifting_w,
    fine_ref,
    coarse_ref,
    arrived,
    region_from,
    lifted,
    chosen,
    picked,
    pool_send,
    pool_recv,
    from_send,
    from_recv,
    lift_send,
    lift_recv,
):
    region, me = lax.axis_index("region"), lax.axis_index("dom")
    partner = lax.rem(region + regions // 2, regions)
    owned = latents_ref.shape[0]
    block = doms * owned

    def part(dom, base=0):
        return pl.ds(base + pl.multiple_of(dom * owned, owned), owned)

    peers = [lax.rem(me + k, doms) for k in range(doms)]
    barrier = pltpu.get_barrier_semaphore()
    for k in range(doms):
        if k:
            pl.semaphore_signal(
                barrier, inc=1, device_id=(region, peers[k]), device_id_type=pl.DeviceIdType.MESH
            )
        pl.semaphore_signal(
            barrier, inc=1, device_id=(partner, peers[k]), device_id_type=pl.DeviceIdType.MESH
        )
    pl.semaphore_wait(barrier, 2 * doms - 1)

    pool = []
    for k in range(doms):
        pool.append(
            to_device(
                partial_ref.at[part(peers[k], block)],
                arrived.at[doms + k],
                pool_send,
                pool_recv,
                doms + k,
                partner,
                peers[k],
            )
        )
        if k:
            pool.append(
                to_device(
                    partial_ref.at[part(peers[k])],
                    arrived.at[k],
                    pool_send,
                    pool_recv,
                    k,
                    region,
                    peers[k],
                )
            )
    for copy in pool:
        copy.start()
    count = senders_ref.shape[0]
    sender_row = senders_ref[...].reshape(1, count) - region * block
    target_row = targets_ref[...].reshape(1, count) - (region * doms + me) * owned
    picked[...] = jnp.concatenate(hot_columns(sender_row, block), axis=1)
    for n in range(window_ref.shape[0] // NODE_TILE):
        rows = pl.ds(n * NODE_TILE, NODE_TILE)
        slots = in_window(window_ref[rows].reshape(1, NODE_TILE), block)
        chosen[rows] = jnp.concatenate(hot_columns(slots, 2 * block), axis=1)
    target_row = hot_rows(target_row, 0, owned)
    total = partial_ref[part(me)].astype(F32)
    for copy in pool:
        copy.wait_recv()
    for k in range(1, 2 * doms):
        total = total + arrived[k].astype(F32)
    start = (latents_ref[...].astype(F32) + mm(total.astype(BF16), pooling_w[...])).astype(BF16)
    region_from[part(me)] = mm(start, sender_w[...]).astype(BF16)
    shares = [
        to_device(
            region_from.at[part(me)], region_from.at[part(me)], from_send, from_recv, k, region, peers[k]
        )
        for k in range(1, doms)
    ]
    for copy in shares:
        copy.start()
    upper_to = mm(start, target_w[...]).astype(BF16)
    to_rows = lax.dot_general(
        target_row, upper_to, (((0,), (0,)), ((), ())), preferred_element_type=F32
    )
    for copy in shares:
        copy.wait_recv()
    message = silu(mm(picked[...], region_from[...]) + to_rows).astype(BF16)
    inflow = mm(target_row, message).astype(BF16)
    result = (start.astype(F32) + normalize(mm(inflow, update_w[...]))).astype(BF16)
    coarse_ref[...] = result
    lifted[part(me)] = mm(result, lifting_w[...]).astype(BF16)
    lifts = []
    for k in range(doms):
        lifts.append(
            to_device(
                lifted.at[part(me)],
                lifted.at[part(me, block)],
                lift_send,
                lift_recv,
                doms + k,
                partner,
                peers[k],
            )
        )
        if k:
            lifts.append(
                to_device(
                    lifted.at[part(me)], lifted.at[part(me)], lift_send, lift_recv, k, region, peers[k]
                )
            )
    for copy in lifts:
        copy.start()
    for copy in pool + shares:
        copy.wait_send()
    for copy in lifts:
        copy.wait_recv()
    for n in range(window_ref.shape[0] // NODE_TILE):
        rows = pl.ds(n * NODE_TILE, NODE_TILE)
        fine_ref[rows] = (
            refined_ref[rows].astype(F32) + mm(chosen[rows], lifted[...])
        ).astype(BF16)
    for copy in lifts:
        copy.wait_send()


def coarse_stage(partial, refined, latents, senders, targets, window_ids, weights, regions, doms):
    whole = pl.BlockSpec(memory_space=pltpu.VMEM)
    nodes, depth = refined.shape
    owned = latents.shape[0]
    block = doms * owned
    count = senders.shape[0]
    pair = [pltpu.SemaphoreType.DMA((2 * doms,))] * 2
    return pl.pallas_call(
        functools.partial(coarse_kernel, regions, doms),
        out_shape=(
            jax.ShapeDtypeStruct((nodes, depth), BF16),
            jax.ShapeDtypeStruct((owned, depth), BF16),
        ),
        in_specs=[whole] * 11,
        out_specs=(whole, whole),
        scratch_shapes=[
            pltpu.VMEM((2 * doms, owned, depth), BF16),
            pltpu.VMEM((block, depth), BF16),
            pltpu.VMEM((2 * block, depth), BF16),
            pltpu.VMEM((nodes, 2 * block), BF16),
            pltpu.VMEM((count, block), BF16),
        ]
        + pair * 3,
        compiler_params=pltpu.CompilerParams(
            collective_id=1, has_side_effects=True, vmem_limit_bytes=48 * 2**20
        ),
    )(
        partial,
        refined,
        latents,
        senders,
        targets,
        window_ids,
        *weights,
    )


def body(
    fine_latents,
    edge_latents,
    send_rows,
    edge_senders,
    edge_targets,
    cluster_ids,
    coarse_latents,
    coarse_senders,
    coarse_targets,
    sender_weight,
    target_weight,
    edge_weight,
    message_weight,
    self_weight,
    inflow_weight,
    update_weight,
    pooling_weight,
    upper_sender,
    upper_target,
    upper_update,
    lifting_weight,
):
    dom_count = lax.axis_size("dom")
    region_count = lax.axis_size("region")
    owned = coarse_latents.shape[0]
    block = dom_count * owned
    halo = halo_stage(fine_latents, send_rows, dom_count)
    refined, partial = fine_stage(
        fine_latents,
        halo,
        edge_latents,
        edge_senders,
        edge_targets,
        cluster_ids,
        2 * block,
        (
            sender_weight,
            target_weight,
            edge_weight,
            message_weight,
            self_weight,
            inflow_weight,
            update_weight,
        ),
    )
    fine_out, coarse_out = coarse_stage(
        partial,
        refined,
        coarse_latents,
        coarse_senders,
        coarse_targets,
        cluster_ids,
        (pooling_weight, upper_sender, upper_target, upper_update, lifting_weight),
        region_count,
        dom_count,
    )
    return (fine_out, coarse_out)


def solution(mesh):
    return jax.shard_map(
        body,
        mesh=mesh,
        in_specs=(
            P(("region", "dom"), None),
            P(("region", "dom"), None),
            P(("region", "dom")),
            P(("region", "dom")),
            P(("region", "dom")),
            P(("region", "dom")),
            P(("region", "dom"), None),
            P(("region", "dom")),
            P(("region", "dom")),
            P(),
            P(),
            P(),
            P(),
            P(),
            P(),
            P(),
            P(),
            P(),
            P(),
            P(),
            P(),
        ),
        out_specs=(P(("region", "dom"), None), P(("region", "dom"), None)),
        check_vma=False,
    )
```

```python
import functools

import jax
import jax.numpy as jnp
from jax import lax
from jax.experimental import pallas as pl
from jax.experimental.pallas import tpu as pltpu
from jax.sharding import PartitionSpec as P

EDGE_TILE = 1024
NODE_TILE = 1024
F32 = jnp.float32
BF16 = jnp.bfloat16


def normalize(values):
    centered = values - jnp.mean(values, axis=-1, keepdims=True)
    variance = jnp.mean(centered * centered, axis=-1, keepdims=True)
    return centered * lax.rsqrt(variance + 1e-05)


def silu(values):
    return values * (0.5 + 0.5 * jnp.tanh(0.5 * values))


def mm(a, b):
    return jnp.dot(a, b, preferred_element_type=F32)


def hot_columns(row, width):
    count = row.shape[1]
    spread = jnp.transpose(jnp.broadcast_to(row, (128, count))).astype(jnp.int16)
    lane = lax.broadcasted_iota(jnp.int32, (count, 128), 1).astype(jnp.int16)
    one = jnp.ones((count, 128), BF16)
    zero = jnp.zeros((count, 128), BF16)
    return [
        jnp.where(spread == lane + jnp.int16(k * 128), one, zero) for k in range(width // 128)
    ]


def hot_rows(row, first, height):
    count = row.shape[1]
    spread = jnp.broadcast_to(row - first, (height, count)).astype(jnp.int16)
    place = lax.broadcasted_iota(jnp.int32, (height, count), 0).astype(jnp.int16)
    return jnp.where(spread == place, jnp.ones((height, count), BF16), jnp.zeros((height, count), BF16))


def in_window(clusters, block):
    within = clusters - lax.axis_index("region") * block
    own = (within >= 0) & (within < block)
    half = lax.axis_size("region") // 2 * block
    return jnp.where(own, within, block + within + jnp.where(within < 0, half, -half))


def fine_kernel(
    edge_steps,
    fine_ref,
    halo_ref,
    edges_ref,
    senders_ref,
    targets_ref,
    window_ref,
    sender_w,
    target_w,
    edge_w,
    message_w,
    self_w,
    inflow_w,
    update_w,
    refined_ref,
    pooled_ref,
    table,
    messages,
    pooled,
):
    step = pl.program_id(0)
    nodes = fine_ref.shape[0]
    extended = nodes + halo_ref.shape[0]
    tile = edges_ref.shape[0]

    @pl.when(step == 0)
    def _():
        table[:nodes] = mm(fine_ref[...], sender_w[...]).astype(BF16)
        table[nodes:extended] = mm(halo_ref[...], sender_w[...]).astype(BF16)
        table[extended : extended + nodes] = mm(fine_ref[...], target_w[...]).astype(BF16)
        table[extended + nodes :] = edge_w[...]
        pooled[...] = jnp.zeros_like(pooled)

    @pl.when(step < edge_steps)
    def _():
        here = pl.ds(pl.multiple_of(step * tile, tile), tile)
        s_row = senders_ref[here].reshape(1, tile)
        t_row = targets_ref[here].reshape(1, tile)
        pieces = hot_columns(s_row, extended) + hot_columns(t_row, nodes) + [edges_ref[...]]
        hidden = silu(mm(jnp.concatenate(pieces, axis=1), table[...])).astype(BF16)
        messages[here] = normalize(
            mm(hidden, message_w[...])
        ).astype(BF16)

    @pl.when(step >= edge_steps)
    def _():
        number = step - edge_steps
        first = pl.multiple_of(number * NODE_TILE, NODE_TILE)
        here = pl.ds(first, NODE_TILE)
        hot = jnp.concatenate(
            [
                hot_rows(targets_ref[pl.ds(k * tile, tile)].reshape(1, tile), first, NODE_TILE)
                for k in range(edge_steps)
            ],
            axis=1,
        )
        inflow = mm(hot, messages[...]).astype(BF16)
        own = fine_ref[here]
        node_hidden = silu(mm(own, self_w[...]) + mm(inflow, inflow_w[...])).astype(BF16)
        refined = (own.astype(F32) + normalize(mm(node_hidden, update_w[...]))).astype(BF16)
        refined_ref[here] = refined
        slots = in_window(window_ref[here].reshape(1, NODE_TILE), pooled.shape[0] // 2)
        pooled[...] += mm(hot_rows(slots, 0, pooled.shape[0]), refined)

    @pl.when(step == pl.num_programs(0) - 1)
    def _():
        pooled_ref[...] = pooled[...].astype(BF16)


def fine_stage(fine, halo, edges, senders, targets, window_ids, window, weights):
    nodes, depth = fine.shape
    count = edges.shape[0]
    edge_steps = count // EDGE_TILE
    node_steps = nodes // NODE_TILE
    whole = pl.BlockSpec(memory_space=pltpu.VMEM)
    return pl.pallas_call(
        functools.partial(fine_kernel, edge_steps),
        grid=(edge_steps + node_steps,),
        out_shape=(
            jax.ShapeDtypeStruct((nodes, depth), BF16),
            jax.ShapeDtypeStruct((window, depth), BF16),
        ),
        in_specs=[
            whole,
            whole,
            pl.BlockSpec((EDGE_TILE, depth), lambda i: (jnp.minimum(i, edge_steps - 1), 0)),
        ]
        + [whole] * 10,
        out_specs=(whole, whole),
        scratch_shapes=[
            pltpu.VMEM((2 * nodes + halo.shape[0] + depth, depth), BF16),
            pltpu.VMEM((count, depth), BF16),
            pltpu.VMEM((window, depth), F32),
        ],
        compiler_params=pltpu.CompilerParams(
            dimension_semantics=("arbitrary",), vmem_limit_bytes=56 * 2**20
        ),
        cost_estimate=pl.CostEstimate(
            flops=2 * depth * count * (3 * nodes + 3 * depth), bytes_accessed=8 * 2**20, transcendentals=0
        ),
    )(
        fine,
        halo,
        edges,
        senders,
        targets,
        window_ids,
        *weights,
    )


def to_device(src, dst, sends, receives, slot, region, dom):
    return pltpu.make_async_remote_copy(
        src_ref=src,
        dst_ref=dst,
        send_sem=sends.at[slot],
        recv_sem=receives.at[slot],
        device_id=(region, dom),
        device_id_type=pl.DeviceIdType.MESH,
    )


def halo_kernel(doms, fine_ref, rows_ref, halo_ref, exported, landed, sends, receives):
    region, me = lax.axis_index("region"), lax.axis_index("dom")
    above, below = lax.rem(me + 1, doms), lax.rem(me + doms - 1, doms)
    barrier = pltpu.get_barrier_semaphore()
    for other in (above, below):
        pl.semaphore_signal(
            barrier, inc=1, device_id=(region, other), device_id_type=pl.DeviceIdType.MESH
        )
    width = rows_ref.shape[0] // 2
    hot = jnp.concatenate(hot_columns(rows_ref[...].reshape(1, -1), fine_ref.shape[0]), axis=1)
    exported[...] = mm(hot, fine_ref[...]).astype(BF16)
    pl.semaphore_wait(barrier, 2)
    lower, upper = pl.ds(0, width), pl.ds(width, width)
    copies = [
        to_device(exported.at[upper], landed.at[lower], sends, receives, 0, region, above),
        to_device(exported.at[lower], landed.at[upper], sends, receives, 1, region, below),
    ]
    for copy in copies:
        copy.start()
    for copy in copies:
        copy.wait()
    zeros = jnp.zeros((width, fine_ref.shape[1]), BF16)
    halo_ref[lower] = jnp.where(me > 0, landed[lower], zeros)
    halo_ref[upper] = jnp.where(me < doms - 1, landed[upper], zeros)


def halo_stage(fine, send_rows, doms):
    whole = pl.BlockSpec(memory_space=pltpu.VMEM)
    shape = (send_rows.shape[0], fine.shape[1])
    return pl.pallas_call(
        functools.partial(halo_kernel, doms),
        out_shape=jax.ShapeDtypeStruct(shape, BF16),
        in_specs=[whole] * 2,
        out_specs=whole,
        scratch_shapes=[
            pltpu.VMEM(shape, BF16),
            pltpu.VMEM(shape, BF16),
            pltpu.SemaphoreType.DMA((2,)),
            pltpu.SemaphoreType.DMA((2,)),
        ],
        compiler_params=pltpu.CompilerParams(
            collective_id=0, has_side_effects=True, vmem_limit_bytes=60 * 2**20
        ),
    )(fine, send_rows)


def coarse_kernel(
    regions,
    doms,
    partial_ref,
    refined_ref,
    latents_ref,
    senders_ref,
    targets_ref,
    window_ref,
    pooling_w,
    sender_w,
    target_w,
    update_w,
    lifting_w,
    fine_ref,
    coarse_ref,
    arrived,
    region_from,
    lifted,
    chosen,
    picked,
    pool_send,
    pool_recv,
    from_send,
    from_recv,
    lift_send,
    lift_recv,
    kept,
    kept_sem,
):
    region, me = lax.axis_index("region"), lax.axis_index("dom")
    partner = lax.rem(region + regions // 2, regions)
    keep = pltpu.make_async_copy(refined_ref, kept, kept_sem)
    keep.start()
    owned = latents_ref.shape[0]
    block = doms * owned

    def part(dom, base=0):
        return pl.ds(base + pl.multiple_of(dom * owned, owned), owned)

    peers = [lax.rem(me + k, doms) for k in range(doms)]
    barrier = pltpu.get_barrier_semaphore()
    for k in range(doms):
        if k:
            pl.semaphore_signal(
                barrier, inc=1, device_id=(region, peers[k]), device_id_type=pl.DeviceIdType.MESH
            )
        pl.semaphore_signal(
            barrier, inc=1, device_id=(partner, peers[k]), device_id_type=pl.DeviceIdType.MESH
        )
    pl.semaphore_wait(barrier, 2 * doms - 1)

    pool = []
    for k in range(doms):
        pool.append(
            to_device(
                partial_ref.at[part(peers[k], block)],
                arrived.at[doms + k],
                pool_send,
                pool_recv,
                doms + k,
                partner,
                peers[k],
            )
        )
        if k:
            pool.append(
                to_device(
                    partial_ref.at[part(peers[k])],
                    arrived.at[k],
                    pool_send,
                    pool_recv,
                    k,
                    region,
                    peers[k],
                )
            )
    for copy in pool:
        copy.start()
    count = senders_ref.shape[0]
    sender_row = senders_ref[...].reshape(1, count) - region * block
    target_row = targets_ref[...].reshape(1, count) - (region * doms + me) * owned
    picked[...] = jnp.concatenate(hot_columns(sender_row, block), axis=1)
    for n in range(window_ref.shape[0] // NODE_TILE):
        rows = pl.ds(n * NODE_TILE, NODE_TILE)
        slots = in_window(window_ref[rows].reshape(1, NODE_TILE), block)
        chosen[rows] = jnp.concatenate(hot_columns(slots, 2 * block), axis=1)
    target_row = hot_rows(target_row, 0, owned)
    total = partial_ref[part(me)].astype(F32)
    for copy in pool:
        copy.wait_recv()
    for k in range(1, 2 * doms):
        total = total + arrived[k].astype(F32)
    start = (latents_ref[...].astype(F32) + mm(total.astype(BF16), pooling_w[...])).astype(BF16)
    region_from[part(me)] = mm(start, sender_w[...]).astype(BF16)
    shares = [
        to_device(
            region_from.at[part(me)], region_from.at[part(me)], from_send, from_recv, k, region, peers[k]
        )
        for k in range(1, doms)
    ]
    for copy in shares:
        copy.start()
    upper_to = mm(start, target_w[...]).astype(BF16)
    to_rows = lax.dot_general(
        target_row, upper_to, (((0,), (0,)), ((), ())), preferred_element_type=F32
    )
    for copy in shares:
        copy.wait_recv()
    message = silu(mm(picked[...], region_from[...]) + to_rows).astype(BF16)
    inflow = mm(target_row, message).astype(BF16)
    result = (start.astype(F32) + normalize(mm(inflow, update_w[...]))).astype(BF16)
    coarse_ref[...] = result
    lifted[part(me)] = mm(result, lifting_w[...]).astype(BF16)
    lifts = []
    for k in range(doms):
        lifts.append(
            to_device(
                lifted.at[part(me)],
                lifted.at[part(me, block)],
                lift_send,
                lift_recv,
                doms + k,
                partner,
                peers[k],
            )
        )
        if k:
            lifts.append(
                to_device(
                    lifted.at[part(me)], lifted.at[part(me)], lift_send, lift_recv, k, region, peers[k]
                )
            )
    for copy in lifts:
        copy.start()
    for copy in pool + shares:
        copy.wait_send()
    keep.wait()
    for copy in lifts:
        copy.wait_recv()
    for n in range(window_ref.shape[0] // NODE_TILE):
        rows = pl.ds(n * NODE_TILE, NODE_TILE)
        fine_ref[rows] = (
            kept[rows].astype(F32) + mm(chosen[rows], lifted[...])
        ).astype(BF16)
    for copy in lifts:
        copy.wait_send()


def coarse_stage(partial, refined, latents, senders, targets, window_ids, weights, regions, doms):
    whole = pl.BlockSpec(memory_space=pltpu.VMEM)
    nodes, depth = refined.shape
    owned = latents.shape[0]
    block = doms * owned
    count = senders.shape[0]
    pair = [pltpu.SemaphoreType.DMA((2 * doms,))] * 2
    return pl.pallas_call(
        functools.partial(coarse_kernel, regions, doms),
        out_shape=(
            jax.ShapeDtypeStruct((nodes, depth), BF16),
            jax.ShapeDtypeStruct((owned, depth), BF16),
        ),
        in_specs=[whole, pl.BlockSpec(memory_space=pl.ANY)] + [whole] * 9,
        out_specs=(whole, whole),
        scratch_shapes=[
            pltpu.VMEM((2 * doms, owned, depth), BF16),
            pltpu.VMEM((block, depth), BF16),
            pltpu.VMEM((2 * block, depth), BF16),
            pltpu.VMEM((nodes, 2 * block), BF16),
            pltpu.VMEM((count, block), BF16),
        ]
        + pair * 3
        + [pltpu.VMEM((nodes, depth), BF16), pltpu.SemaphoreType.DMA],
        compiler_params=pltpu.CompilerParams(
            collective_id=1, has_side_effects=True, vmem_limit_bytes=60 * 2**20
        ),
    )(
        partial,
        refined,
        latents,
        senders,
        targets,
        window_ids,
        *weights,
    )


def body(
    fine_latents,
    edge_latents,
    send_rows,
    edge_senders,
    edge_targets,
    cluster_ids,
    coarse_latents,
    coarse_senders,
    coarse_targets,
    sender_weight,
    target_weight,
    edge_weight,
    message_weight,
    self_weight,
    inflow_weight,
    update_weight,
    pooling_weight,
    upper_sender,
    upper_target,
    upper_update,
    lifting_weight,
):
    dom_count = lax.axis_size("dom")
    region_count = lax.axis_size("region")
    owned = coarse_latents.shape[0]
    block = dom_count * owned
    halo = halo_stage(fine_latents, send_rows, dom_count)
    refined, partial = fine_stage(
        fine_latents,
        halo,
        edge_latents,
        edge_senders,
        edge_targets,
        cluster_ids,
        2 * block,
        (
            sender_weight,
            target_weight,
            edge_weight,
            message_weight,
            self_weight,
            inflow_weight,
            update_weight,
        ),
    )
    fine_out, coarse_out = coarse_stage(
        partial,
        refined,
        coarse_latents,
        coarse_senders,
        coarse_targets,
        cluster_ids,
        (pooling_weight, upper_sender, upper_target, upper_update, lifting_weight),
        region_count,
        dom_count,
    )
    return (fine_out, coarse_out)


def solution(mesh):
    return jax.shard_map(
        body,
        mesh=mesh,
        in_specs=(
            P(("region", "dom"), None),
            P(("region", "dom"), None),
            P(("region", "dom")),
            P(("region", "dom")),
            P(("region", "dom")),
            P(("region", "dom")),
            P(("region", "dom"), None),
            P(("region", "dom")),
            P(("region", "dom")),
            P(),
            P(),
            P(),
            P(),
            P(),
            P(),
            P(),
            P(),
            P(),
            P(),
            P(),
            P(),
        ),
        out_specs=(P(("region", "dom"), None), P(("region", "dom"), None)),
        check_vma=False,
    )
```
